512 devices in a mesh: dp: 4 (over x_lo, core), expert: 16 (over z), tensor: 8 (over x_hi, y).
Axes of the slice: x: 4 (x_hi: 2, x_lo: 2; x = x_hi * 2 + x_lo), y: 4, z: 16, core: 2. Of those that a mesh axis runs over, the one named last changes fastest.
Arguments:
- tokens: bfloat16 [8192, 2048], P(('dp', 'expert')), may hold values from -6 to 6
- routes: int32 [8192], P(('dp', 'expert')), may hold values from 0 to 15, as said below
- slots: int32 [8192], P(('dp', 'expert')), may hold values from 0 to 16, as said below
- gate: float32 [8192], P(('dp', 'expert')), may hold values from 0.25 to 1
- cotangent: bfloat16 [8192, 2048], P(('dp', 'expert')), may hold values from -6 to 6
- w_in: bfloat16 [16, 2048, 8192], P('expert', 'dp', 'tensor'), may hold values from -0.125 to 0.125
- w_out: bfloat16 [16, 8192, 2048], P('expert', 'tensor', 'dp'), may hold values from -0.0625 to 0.0625
Outputs:
- grad_tokens: bfloat16 [8192, 2048], P(('dp', 'expert'))
- grad_w_in: bfloat16 [16, 2048, 8192], P('expert', 'dp', 'tensor')
- grad_w_out: bfloat16 [16, 8192, 2048], P('expert', 'tensor', 'dp')
The draws below stay inside these ranges and needn't reach their ends.
Inputs may be any that keep to these rules, and one draw needn't show every extreme that they name: `routes`: in the 128 tokens of every group (rows held by one index of dp+expert) every expert is named; in every data replica one expert is named by more than 16 tokens of each of its groups. The kept tokens of one group and one expert take slots 0, 1, 2, ... in token order; the value 16 marks a dropped token, and every group drops some token.
All inputs are finite; a program needn't handle non-finite values.
Results may differ from the reference program's by a relative error of at most 0.0058.
Values may be sent and summed in bfloat16 or wider, within the bound.
No kernel may reach another device: no remote copies, remote signals or barrier semaphores. Data moves between devices by JAX's collectives and lax.ppermute only.
A program may use at most 64 MiB of HBM per device.

```python
import jax
import jax.numpy as jnp
from jax import lax

D = 2048
FF = 8192
TOK_GRP = 128
EXPERTS = 16
CAP = 16
TOKENS = 8192


def route_plan(key):
    groups = TOKENS // TOK_GRP
    replicas = groups // EXPERTS
    key_hot = jax.random.fold_in(key, 11)
    key_pick = jax.random.fold_in(key, 12)
    key_order = jax.random.fold_in(key, 13)
    key_weight = jax.random.fold_in(key, 14)
    hot_expert = jax.random.randint(key_hot, (replicas,), 0, EXPERTS)
    favoured = max(EXPERTS // 4, 1)
    ranked = jax.random.permutation(key_weight, EXPERTS)
    weights = jnp.where(ranked < favoured, 4, 1).astype(jnp.int32)
    bounds = jnp.cumsum(weights)
    weight_total = 4 * favoured + EXPERTS - favoured
    picks = jax.random.randint(key_pick, (groups, TOK_GRP), 0, weight_total)
    chosen = jnp.sum((picks[:, :, None] >= bounds[None, None, :]).astype(jnp.int32), axis=-1)
    scores = jax.random.randint(key_order, (groups, TOK_GRP), 0, 1 << 20) * TOK_GRP
    scores = scores + jnp.arange(TOK_GRP, dtype=jnp.int32)[None, :]
    position_rank = jnp.argsort(jnp.argsort(scores, axis=1), axis=1).astype(jnp.int32)
    group_hot = jnp.repeat(hot_expert, EXPERTS)
    covering = position_rank - (CAP + 1)
    routes = jnp.where(position_rank < CAP + 1, group_hot[:, None], jnp.where(covering < EXPERTS, covering, chosen))
    routes = routes.astype(jnp.int32)
    one_hot = (routes[:, :, None] == jnp.arange(EXPERTS, dtype=jnp.int32)[None, None, :]).astype(jnp.int32)
    before = jnp.cumsum(one_hot, axis=1) - one_hot
    earlier = jnp.sum(before * one_hot, axis=-1)
    slots = jnp.minimum(earlier, CAP).astype(jnp.int32)
    return (routes.reshape(TOKENS), slots.reshape(TOKENS))


def draw_routes(key, part):
    plan = route_plan(key)
    return plan[0]


def draw_slots(key, part):
    plan = route_plan(key)
    return plan[1]


def block_levels(key, dims, split, least, largest):
    level, own = 1.0, jax.random.fold_in(key, 6)
    for axis_at, parts in split:
        heights = jnp.exp(jax.random.uniform(jax.random.fold_in(own, axis_at), (parts,), jnp.float32, least / len(split), largest / len(split)))
        level = level * jnp.repeat(heights, dims[axis_at] // parts).reshape([-1 if axis == axis_at else 1 for axis in range(len(dims))])
    return level


def scatter_about(rng, dims, deviation, bound, shards=(), held_as=jnp.bfloat16):
    entries = deviation * jax.random.normal(rng, dims, jnp.float32)
    if shards:
        entries = entries * block_levels(rng, dims, shards, -0.22, 0.18)
    return jnp.clip(entries, -bound, bound).astype(held_as)


def setup_inputs(seed: int = 0) -> dict:
    seeds = jax.random.split(jax.random.key(seed), 8)
    return {
        "tokens": scatter_about(seeds[0], (TOKENS, D), 1.0, 6.0, ((0, 64),)),
        "routes": draw_routes(jax.random.fold_in(seeds[7], 71), 0),
        "slots": draw_slots(jax.random.fold_in(seeds[7], 71), 0),
        "gate": jnp.clip(0.25 + 0.75 * jax.random.uniform(seeds[3], (TOKENS,), jnp.float32) ** block_levels(seeds[3], (TOKENS,), ((0, 64),), -0.2, 0.2), 0.25, 1.0),
        "cotangent": scatter_about(seeds[4], (TOKENS, D), 1.0, 6.0, ((0, 64),)),
        "w_in": scatter_about(seeds[5], (EXPERTS, D, FF), D ** -0.5, 0.125, ((0, 16), (1, 4), (2, 8))),
        "w_out": scatter_about(seeds[6], (EXPERTS, FF, D), FF ** -0.5, 0.0625, ((0, 16), (1, 8), (2, 4))),
    }


def gelu_parts(preact):
    normal_cdf = 0.5 * (1.0 + jax.scipy.special.erf(preact * 0.7071067811865476))
    density = jnp.exp(-0.5 * preact * preact) * 0.3989422804014327
    return preact * normal_cdf, normal_cdf + preact * density


def expert_step(operands):
    token_rows, grad_rows, first_weight, second_weight = operands
    preact = jnp.dot(token_rows, first_weight, preferred_element_type=jnp.float32)
    value, slope = gelu_parts(preact)
    hidden = value.astype(jnp.bfloat16)
    grad_hidden = jnp.dot(grad_rows, second_weight.T, preferred_element_type=jnp.float32)
    grad_pre = (grad_hidden * slope).astype(jnp.bfloat16)
    grad_first = jnp.dot(token_rows.T, grad_pre, preferred_element_type=jnp.float32).astype(jnp.bfloat16)
    grad_second = jnp.dot(hidden.T, grad_rows, preferred_element_type=jnp.float32).astype(jnp.bfloat16)
    row_grads = jnp.dot(grad_pre, first_weight.T, preferred_element_type=jnp.float32).astype(jnp.bfloat16)
    return grad_first, grad_second, row_grads


def reference(tokens, routes, slots, gate, cotangent, w_in, w_out):
    replicas = TOKENS // (TOK_GRP * EXPERTS)
    buffer_rows = replicas * EXPERTS * EXPERTS * CAP
    token_ids = jnp.arange(TOKENS, dtype=jnp.int32)
    group = token_ids // TOK_GRP
    replica = group // EXPERTS
    source = group % EXPERTS
    is_kept = slots < CAP
    position = ((replica * EXPERTS + routes) * EXPERTS + source) * CAP + slots
    position = jnp.where(is_kept, position, buffer_rows).astype(jnp.int32)
    scaled = (cotangent.astype(jnp.float32) * gate[:, None]).astype(jnp.bfloat16)
    token_buffer = jnp.zeros((buffer_rows, D), jnp.bfloat16).at[position].set(tokens, mode="drop")
    grad_buffer = jnp.zeros((buffer_rows, D), jnp.bfloat16).at[position].set(scaled, mode="drop")
    token_buffer = token_buffer.reshape(replicas, EXPERTS, EXPERTS * CAP, D).transpose(1, 0, 2, 3)
    token_buffer = token_buffer.reshape(EXPERTS, replicas * EXPERTS * CAP, D)
    grad_buffer = grad_buffer.reshape(replicas, EXPERTS, EXPERTS * CAP, D).transpose(1, 0, 2, 3)
    grad_buffer = grad_buffer.reshape(EXPERTS, replicas * EXPERTS * CAP, D)
    grad_w_in, grad_w_out, row_grads = lax.map(expert_step, (token_buffer, grad_buffer, w_in, w_out))
    row_grads = row_grads.reshape(EXPERTS, replicas, EXPERTS * CAP, D).transpose(1, 0, 2, 3)
    row_grads = row_grads.reshape(buffer_rows, D)
    picked = jnp.take(row_grads, jnp.minimum(position, buffer_rows - 1).astype(jnp.int32), axis=0)
    grad_tokens = jnp.where(is_kept[:, None], picked, jnp.zeros_like(picked))
    return grad_tokens, grad_w_in, grad_w_out
```

```python
import jax
import jax.numpy as jnp
from jax import lax
from jax.experimental import pallas as pl
from jax.experimental.pallas import tpu as pltpu
from jax.sharding import PartitionSpec as P

ACROSS = [(0, 2), (2, 0), (1, 3), (3, 1)]
BESIDE = [(0, 1), (1, 0), (2, 3), (3, 2)]
DIAGONAL = [(0, 3), (3, 0), (1, 2), (2, 1)]
VMEM_BYTES = 48 * 1024 * 1024


def gelu_parts(preact):
    normal_cdf = 0.5 * (1.0 + lax.erf(preact * 0.7071067811865476))
    density = jnp.exp(-0.5 * preact * preact) * 0.3989422804014327
    return (preact * normal_cdf, normal_cdf + preact * density)


def route_table(routes, slots, experts_count, capacity):
    position = jnp.where(slots < capacity, routes * capacity + slots, -1)
    targets = lax.broadcasted_iota(jnp.int32, (experts_count * capacity, routes.shape[0]), 0)
    return (targets == position[None, :]).astype(jnp.bfloat16)


def dot(left, right, left_dim, right_dim):
    return lax.dot_general(
        left,
        right,
        (((left_dim,), (right_dim,)), ((), ())),
        preferred_element_type=jnp.float32,
    )


def hidden_kernel(rows_ref, *refs):
    first, second = refs[0:4], refs[4:8]
    acts_ref, sent_ref, total = refs[8:11]
    step, steps = pl.program_id(0), pl.num_programs(0)
    block = rows_ref.shape[3]
    halves = first[0].shape[0] // block
    blocks = range(rows_ref.shape[0])

    def weight_in(t):
        return first[t // halves][pl.ds((t % halves) * block, block), :]

    def weight_out(t):
        return second[t // halves][:, pl.ds((t % halves) * block, block)]

    preact = sum(dot(rows_ref[t, 0], weight_in(t), 1, 0) for t in blocks)
    grad_hidden = sum(dot(rows_ref[t, 1], weight_out(t), 1, 1) for t in blocks)
    value, slope = gelu_parts(preact)
    grad_pre = (grad_hidden * slope).astype(jnp.bfloat16)
    acts_ref[0] = value.astype(jnp.bfloat16)
    acts_ref[1] = grad_pre

    @pl.when(step == 0)
    def _():
        for t in blocks:
            total[t] = dot(grad_pre, weight_in(t), 1, 1)

    @pl.when(step > 0)
    def _():
        for t in blocks:
            total[t] += dot(grad_pre, weight_in(t), 1, 1)

    @pl.when(step == steps - 1)
    def _():
        sent_ref[...] = total[...].astype(jnp.bfloat16)


def hidden_layer(rows, first, second):
    blocks, _, count, block = rows.shape
    depth, width = first[0].shape
    tile = 256
    flops = 3 * 2 * count * blocks * block * width
    return pl.pallas_call(
        hidden_kernel,
        grid=(width // tile,),
        in_specs=[pl.BlockSpec(rows.shape, lambda j: (0, 0, 0, 0))]
        + [pl.BlockSpec((depth, tile), lambda j: (0, j))] * 4
        + [pl.BlockSpec((tile, depth), lambda j: (j, 0))] * 4,
        out_specs=[
            pl.BlockSpec((2, count, tile), lambda j: (0, 0, j)),
            pl.BlockSpec((blocks, count, block), lambda j: (0, 0, 0)),
        ],
        out_shape=[
            jax.ShapeDtypeStruct((2, count, width), jnp.bfloat16),
            jax.ShapeDtypeStruct((blocks, count, block), jnp.bfloat16),
        ],
        scratch_shapes=[pltpu.VMEM((blocks, count, block), jnp.float32)],
        compiler_params=pltpu.CompilerParams(vmem_limit_bytes=VMEM_BYTES),
        cost_estimate=pl.CostEstimate(
            flops=flops, bytes_accessed=13 * 1024 * 1024, transcendentals=2 * count * width
        ),
        name="hidden_layer",
    )(rows, *first, *second)


def weights_kernel(*refs):
    rows, acts = refs[0:4], refs[4:8]
    first_ref, second_ref = refs[8:10]
    block = rows[0].shape[3]
    for b in range(rows[0].shape[0]):
        first_ref[pl.ds(b * block, block), :] = sum(
            dot(rows[k][b, 0], acts[k][1], 0, 0) for k in range(4)
        ).astype(jnp.bfloat16)
        second_ref[:, pl.ds(b * block, block)] = sum(
            dot(acts[k][0], rows[k][b, 1], 0, 0) for k in range(4)
        ).astype(jnp.bfloat16)


def weight_grads(rows, acts):
    _, _, count, block = rows[0].shape
    width = acts[0].shape[2]
    tile, depth = 256, 2 * block
    flops = 2 * 2 * 4 * count * depth * width
    return pl.pallas_call(
        weights_kernel,
        grid=(width // tile,),
        in_specs=[pl.BlockSpec((2, 2, count, block), lambda j: (0, 0, 0, 0))] * 4
        + [pl.BlockSpec((2, count, tile), lambda j: (0, 0, j))] * 4,
        out_specs=[
            pl.BlockSpec((depth, tile), lambda j: (0, j)),
            pl.BlockSpec((tile, depth), lambda j: (j, 0)),
        ],
        out_shape=[
            jax.ShapeDtypeStruct((depth, width), jnp.bfloat16),
            jax.ShapeDtypeStruct((width, depth), jnp.bfloat16),
        ],
        compiler_params=pltpu.CompilerParams(vmem_limit_bytes=VMEM_BYTES),
        cost_estimate=pl.CostEstimate(
            flops=flops, bytes_accessed=8 * 1024 * 1024, transcendentals=0
        ),
        name="weight_grads",
    )(*rows, *acts)


def shards(tokens, routes, slots, gate, cotangent, w_in, w_out):
    experts = lax.axis_size("expert")
    parts = lax.axis_size("tensor")
    group, model_width = tokens.shape
    capacity = 2 * group // experts
    count = experts * capacity
    block = model_width // parts
    replica = lax.axis_index("dp")
    part = lax.axis_index("tensor")
    halves = parts // 4

    start = ((replica ^ (part // halves)) * halves + part % halves) * block
    own_tokens = lax.dynamic_slice_in_dim(tokens, start, block, 1)
    own_cotangent = lax.dynamic_slice_in_dim(cotangent, start, block, 1)
    scaled = (own_cotangent.astype(jnp.float32) * gate[:, None]).astype(jnp.bfloat16)
    table = route_table(routes, slots, experts, capacity)
    sent_tokens = dot(table, own_tokens, 1, 0).astype(jnp.bfloat16)
    sent_grads = dot(table, scaled, 1, 0).astype(jnp.bfloat16)
    sent = jnp.concatenate(
        [
            sent_tokens.reshape(experts, capacity, block),
            sent_grads.reshape(experts, capacity, block),
        ],
        axis=1,
    )
    came = lax.all_to_all(sent, "expert", 0, 0, tiled=True)
    came = came.reshape(experts, 2, capacity, block).transpose(1, 0, 2, 3)
    came = came.reshape(2, count, block)
    rows = lax.all_to_all(
        jnp.broadcast_to(came[None], (parts, 2, count, block)), "tensor", 0, 0, tiled=True
    )

    first0, second0 = w_in[0], w_out[0]
    first2, second2 = lax.ppermute(first0, "dp", ACROSS), lax.ppermute(second0, "dp", ACROSS)
    first1, second1 = lax.ppermute(first0, "dp", BESIDE), lax.ppermute(second0, "dp", BESIDE)
    first3, second3 = lax.ppermute(first2, "dp", BESIDE), lax.ppermute(second2, "dp", BESIDE)

    acts0, partial_rows = hidden_layer(
        rows, (first0, first1, first2, first3), (second0, second1, second2, second3)
    )

    terms = lax.all_to_all(partial_rows, "tensor", 0, 0, tiled=True)
    row_grads = jnp.sum(terms.astype(jnp.float32), axis=0).astype(jnp.bfloat16)
    returned = lax.all_to_all(
        row_grads.reshape(experts, capacity, block), "expert", 0, 0, tiled=True
    ).reshape(count, block)
    own_grads = dot(table, returned, 0, 0).astype(jnp.bfloat16)
    pieces = lax.all_to_all(
        jnp.broadcast_to(own_grads[None], (parts, group, block)), "tensor", 0, 0, tiled=True
    )
    pieces = pieces.reshape(2, 2, halves, group, block)
    pieces = jnp.where(replica // 2 == 1, pieces[::-1], pieces)
    pieces = jnp.where(replica % 2 == 1, pieces[:, ::-1], pieces)
    grad_tokens = pieces.reshape(parts, group, block).transpose(1, 0, 2).reshape(group, model_width)

    rows1 = lax.ppermute(rows[halves : 2 * halves], "dp", BESIDE)
    rows2 = lax.ppermute(rows[2 * halves : 3 * halves], "dp", ACROSS)
    rows3 = lax.ppermute(rows[3 * halves :], "dp", DIAGONAL)
    acts2 = lax.ppermute(acts0, "dp", ACROSS)
    acts1 = lax.ppermute(acts0, "dp", BESIDE)
    acts3 = lax.ppermute(acts2, "dp", BESIDE)
    grad_first, grad_second = weight_grads((rows, rows1, rows2, rows3), (acts0, acts1, acts2, acts3))
    return grad_tokens, grad_first[None], grad_second[None]


def solution(mesh):
    return jax.shard_map(
        shards,
        mesh=mesh,
        in_specs=(
            P(("dp", "expert"), None),
            P(("dp", "expert")),
            P(("dp", "expert")),
            P(("dp", "expert")),
            P(("dp", "expert"), None),
            P("expert", "dp", "tensor"),
            P("expert", "tensor", "dp"),
        ),
        out_specs=(
            P(("dp", "expert"), None),
            P("expert", "dp", "tensor"),
            P("expert", "tensor", "dp"),
        ),
        check_vma=False,
    )
```

```python
import jax
import jax.numpy as jnp
from jax import lax
from jax.experimental import pallas as pl
from jax.experimental.pallas import tpu as pltpu
from jax.sharding import PartitionSpec as P

ACROSS = [(0, 2), (2, 0), (1, 3), (3, 1)]
DIAGONAL = [(0, 3), (3, 0), (1, 2), (2, 1)]
BESIDE = [(0, 1), (1, 0), (2, 3), (3, 2)]
TILE = 1024
VMEM_BYTES = 24 * 1024 * 1024


def gelu_parts(preact):
    normal_cdf = 0.5 * (1.0 + lax.erf(preact * 0.7071067811865476))
    density = jnp.exp(-0.5 * preact * preact) * 0.3989422804014327
    return (preact * normal_cdf, normal_cdf + preact * density)


def route_table(routes, slots, experts_count, capacity):
    position = jnp.where(slots < capacity, routes * capacity + slots, -1)
    targets = lax.broadcasted_iota(jnp.int32, (experts_count * capacity, routes.shape[0]), 0)
    return (targets == position[None, :]).astype(jnp.bfloat16)


def dot(left, right, left_dim, right_dim):
    return lax.dot_general(
        left,
        right,
        (((left_dim,), (right_dim,)), ((), ())),
        preferred_element_type=jnp.float32,
    )


def hidden_kernel(place_ref, rows_ref, *refs):
    first, second = refs[0:4], refs[4:8]
    acts_ref, sent_ref, total = refs[8:11]
    step, steps = pl.program_id(0), pl.num_programs(0)
    block = sent_ref.shape[2]
    halves = first[0].shape[0] // block

    preact = sum(dot(rows_ref[k, 0], first[k][...], 1, 0) for k in range(4))
    grad_hidden = sum(dot(rows_ref[k, 1], second[k][...], 1, 1) for k in range(4))
    value, slope = gelu_parts(preact)
    grad_pre = (grad_hidden * slope).astype(jnp.bfloat16)
    acts_ref[0] = value.astype(jnp.bfloat16)
    acts_ref[1] = grad_pre

    @pl.when(step == 0)
    def _():
        total[...] = jnp.zeros_like(total)

    for t in range(4 * halves):
        weight = first[t // halves][pl.ds((t % halves) * block, block), :]
        total[t] += dot(grad_pre, weight, 1, 1)

    @pl.when(step == steps - 1)
    def _():
        for t in range(4 * halves):
            sent_ref[place_ref[t]] = total[t].astype(jnp.bfloat16)


def hidden_layer(places, rows, first, second):
    _, _, count, depth = rows.shape
    width = first[0].shape[1]
    parts = places.shape[0]
    block = 4 * depth // parts
    spec = pltpu.PrefetchScalarGridSpec(
        num_scalar_prefetch=1,
        grid=(width // TILE,),
        in_specs=[pl.BlockSpec(rows.shape, lambda j, _: (0, 0, 0, 0))]
        + [pl.BlockSpec((depth, TILE), lambda j, _: (0, j))] * 4
        + [pl.BlockSpec((TILE, depth), lambda j, _: (j, 0))] * 4,
        out_specs=[
            pl.BlockSpec((2, count, TILE), lambda j, _: (0, 0, j)),
            pl.BlockSpec((parts, count, block), lambda j, _: (0, 0, 0)),
        ],
        scratch_shapes=[pltpu.VMEM((parts, count, block), jnp.float32)],
    )
    return pl.pallas_call(
        hidden_kernel,
        grid_spec=spec,
        out_shape=[
            jax.ShapeDtypeStruct((2, count, width), jnp.bfloat16),
            jax.ShapeDtypeStruct((parts, count, block), jnp.bfloat16),
        ],
        compiler_params=pltpu.CompilerParams(vmem_limit_bytes=VMEM_BYTES),
        cost_estimate=pl.CostEstimate(
            flops=24 * count * depth * width,
            bytes_accessed=24 * count * depth * 4,
            transcendentals=2 * count * width,
        ),
        name="hidden_layer",
    )(places, rows, *first, *second)


def total_kernel(terms_ref, out_ref):
    out_ref[...] = jnp.sum(terms_ref[...].astype(jnp.float32), axis=0).astype(jnp.bfloat16)


def total_rows(terms):
    parts, count, block = terms.shape
    tile = count // 2
    return pl.pallas_call(
        total_kernel,
        grid=(count // tile,),
        in_specs=[pl.BlockSpec((parts, tile, block), lambda j: (0, j, 0))],
        out_specs=pl.BlockSpec((tile, block), lambda j: (j, 0)),
        out_shape=jax.ShapeDtypeStruct((count, block), jnp.bfloat16),
        name="total_rows",
    )(terms)


def join_kernel(pieces_ref, out_ref):
    parts, _, block = pieces_ref.shape
    for t in range(parts):
        out_ref[:, pl.ds(t * block, block)] = pieces_ref[t]


def join_columns(pieces):
    parts, group, block = pieces.shape
    return pl.pallas_call(
        join_kernel,
        out_shape=jax.ShapeDtypeStruct((group, parts * block), jnp.bfloat16),
        name="join_columns",
    )(pieces)


def weights_kernel(*refs):
    rows, acts = refs[0:4], refs[4:8]
    first_ref, second_ref = refs[8:10]
    first_ref[...] = sum(dot(rows[k][0], acts[k][1], 0, 0) for k in range(4)).astype(jnp.bfloat16)
    second_ref[...] = sum(dot(acts[k][0], rows[k][1], 0, 0) for k in range(4)).astype(jnp.bfloat16)


def weight_grads(rows, acts):
    _, _, count, depth = rows[0].shape
    width = acts[0].shape[2]
    return pl.pallas_call(
        weights_kernel,
        grid=(width // TILE,),
        in_specs=[pl.BlockSpec((None, 2, count, depth), lambda j: (0, 0, 0, 0))] * 4
        + [pl.BlockSpec((2, count, TILE), lambda j: (0, 0, j))] * 4,
        out_specs=[
            pl.BlockSpec((depth, TILE), lambda j: (0, j)),
            pl.BlockSpec((TILE, depth), lambda j: (j, 0)),
        ],
        out_shape=[
            jax.ShapeDtypeStruct((depth, width), jnp.bfloat16),
            jax.ShapeDtypeStruct((width, depth), jnp.bfloat16),
        ],
        compiler_params=pltpu.CompilerParams(vmem_limit_bytes=VMEM_BYTES),
        cost_estimate=pl.CostEstimate(
            flops=16 * count * depth * width,
            bytes_accessed=8 * 1024 * 1024,
            transcendentals=0,
        ),
        name="weight_grads",
    )(*rows, *acts)


def shards(tokens, routes, slots, gate, cotangent, w_in, w_out):
    experts = lax.axis_size("expert")
    parts = lax.axis_size("tensor")
    ring = lax.axis_size("dp")
    group, model_width = tokens.shape
    capacity = 2 * group // experts
    count = experts * capacity
    block = model_width // parts
    depth = model_width // ring
    halves = parts // ring
    replica = lax.axis_index("dp").astype(jnp.int32)
    y = lax.axis_index("tensor").astype(jnp.int32) % ring
    rings = [[i * ring + j for j in range(ring)] for i in range(halves)]

    start = (replica ^ y) * depth
    own_tokens = lax.dynamic_slice_in_dim(tokens, start, depth, 1)
    own_cotangent = lax.dynamic_slice_in_dim(cotangent, start, depth, 1)
    scaled = (own_cotangent.astype(jnp.float32) * gate[:, None]).astype(jnp.bfloat16)
    table = route_table(routes, slots, experts, capacity)
    sent_tokens = dot(table, own_tokens, 1, 0).astype(jnp.bfloat16)
    sent_grads = dot(table, scaled, 1, 0).astype(jnp.bfloat16)
    sent = jnp.concatenate(
        [
            sent_tokens.reshape(experts, capacity, depth),
            sent_grads.reshape(experts, capacity, depth),
        ],
        axis=1,
    )
    came = lax.all_to_all(sent, "expert", 0, 0, tiled=True)
    came = came.reshape(experts, 2, capacity, depth).transpose(1, 0, 2, 3)
    copies = jnp.broadcast_to(came.reshape(1, 2, count, depth), (ring, 2, count, depth))
    rows = lax.all_to_all(copies, "tensor", 0, 0, axis_index_groups=rings, tiled=True)

    first0, second0 = w_in[0], w_out[0]
    first2, second2 = lax.ppermute(first0, "dp", ACROSS), lax.ppermute(second0, "dp", ACROSS)
    first1, second1 = lax.ppermute(first0, "dp", BESIDE), lax.ppermute(second0, "dp", BESIDE)
    first3, second3 = lax.ppermute(first2, "dp", BESIDE), lax.ppermute(second2, "dp", BESIDE)

    order = jnp.arange(parts, dtype=jnp.int32)
    places = ((order // halves) ^ replica) * halves + order % halves
    acts0, partial_rows = hidden_layer(
        places, rows, (first0, first1, first2, first3), (second0, second1, second2, second3)
    )

    rows1 = lax.ppermute(rows[1:2], "dp", BESIDE)
    rows2 = lax.ppermute(rows[2:3], "dp", ACROSS)
    rows3 = lax.ppermute(rows[3:4], "dp", DIAGONAL)
    acts1 = lax.ppermute(acts0, "dp", BESIDE)
    acts2 = lax.ppermute(acts0, "dp", ACROSS)
    partial_rows, rows2 = lax.optimization_barrier((partial_rows, rows2))
    terms = lax.all_to_all(partial_rows, "tensor", 0, 0, tiled=True)
    row_grads = total_rows(terms)
    row_grads, rows1, acts1 = lax.optimization_barrier((row_grads, rows1, acts1))
    returned = lax.all_to_all(
        row_grads.reshape(experts, capacity, block), "expert", 0, 0, tiled=True
    ).reshape(count, block)
    own_grads = dot(table, returned, 0, 0).astype(jnp.bfloat16)
    own_grads, acts2, rows3 = lax.optimization_barrier((own_grads, acts2, rows3))
    acts3 = lax.ppermute(acts2, "dp", BESIDE)
    pieces = lax.all_to_all(
        jnp.broadcast_to(own_grads[None], (parts, group, block)), "tensor", 0, 0, tiled=True
    )
    grad_first, grad_second = weight_grads((rows, rows1, rows2, rows3), (acts0, acts1, acts2, acts3))
    pieces, grad_first, grad_second = lax.optimization_barrier((pieces, grad_first, grad_second))
    grad_tokens = join_columns(pieces)
    return grad_tokens, grad_first[None], grad_second[None]


def solution(mesh):
    return jax.shard_map(
        shards,
        mesh=mesh,
        in_specs=(
            P(("dp", "expert"), None),
            P(("dp", "expert")),
            P(("dp", "expert")),
            P(("dp", "expert")),
            P(("dp", "expert"), None),
            P("expert", "dp", "tensor"),
            P("expert", "tensor", "dp"),
        ),
        out_specs=(
            P(("dp", "expert"), None),
            P("expert", "dp", "tensor"),
            P("expert", "tensor", "dp"),
        ),
        check_vma=False,
    )
```

```python
import jax
import jax.numpy as jnp
from jax import lax
from jax.experimental import pallas as pl
from jax.experimental.pallas import tpu as pltpu
from jax.sharding import PartitionSpec as P

ACROSS = [(0, 2), (2, 0), (1, 3), (3, 1)]
BESIDE = [(0, 1), (1, 0), (2, 3), (3, 2)]
TILE = 1024
VMEM_BYTES = 24 * 1024 * 1024


def gelu_parts(preact):
    normal_cdf = 0.5 * (1.0 + lax.erf(preact * 0.7071067811865476))
    density = jnp.exp(-0.5 * preact * preact) * 0.3989422804014327
    return (preact * normal_cdf, normal_cdf + preact * density)


def route_table(routes, slots, experts_count, capacity):
    position = jnp.where(slots < capacity, routes * capacity + slots, -1)
    targets = lax.broadcasted_iota(jnp.int32, (experts_count * capacity, routes.shape[0]), 0)
    return (targets == position[None, :]).astype(jnp.bfloat16)


def dot(left, right, left_dim, right_dim):
    return lax.dot_general(
        left,
        right,
        (((left_dim,), (right_dim,)), ((), ())),
        preferred_element_type=jnp.float32,
    )


def hidden_kernel(place_ref, rows_ref, *refs):
    first, second = refs[0:4], refs[4:8]
    acts_ref, sent_ref, total = refs[8:11]
    step, steps = pl.program_id(0), pl.num_programs(0)
    block = sent_ref.shape[2]
    halves = first[0].shape[0] // block

    preact = sum(dot(rows_ref[k, 0], first[k][...], 1, 0) for k in range(4))
    grad_hidden = sum(dot(rows_ref[k, 1], second[k][...], 1, 1) for k in range(4))
    value, slope = gelu_parts(preact)
    grad_pre = (grad_hidden * slope).astype(jnp.bfloat16)
    acts_ref[0] = value.astype(jnp.bfloat16)
    acts_ref[1] = grad_pre

    @pl.when(step == 0)
    def _():
        total[...] = jnp.zeros_like(total)

    for t in range(4 * halves):
        weight = first[t // halves][pl.ds((t % halves) * block, block), :]
        total[t] += dot(grad_pre, weight, 1, 1)

    @pl.when(step == steps - 1)
    def _():
        for t in range(4 * halves):
            sent_ref[place_ref[t]] = total[t].astype(jnp.bfloat16)


def hidden_layer(places, rows, first, second):
    _, _, count, depth = rows.shape
    width = first[0].shape[1]
    parts = places.shape[0]
    block = 4 * depth // parts
    spec = pltpu.PrefetchScalarGridSpec(
        num_scalar_prefetch=1,
        grid=(width // TILE,),
        in_specs=[pl.BlockSpec(rows.shape, lambda j, _: (0, 0, 0, 0))]
        + [pl.BlockSpec((depth, TILE), lambda j, _: (0, j))] * 4
        + [pl.BlockSpec((TILE, depth), lambda j, _: (j, 0))] * 4,
        out_specs=[
            pl.BlockSpec((2, count, TILE), lambda j, _: (0, 0, j)),
            pl.BlockSpec((parts, count, block), lambda j, _: (0, 0, 0)),
        ],
        scratch_shapes=[pltpu.VMEM((parts, count, block), jnp.float32)],
    )
    return pl.pallas_call(
        hidden_kernel,
        grid_spec=spec,
        out_shape=[
            jax.ShapeDtypeStruct((2, count, width), jnp.bfloat16),
            jax.ShapeDtypeStruct((parts, count, block), jnp.bfloat16),
        ],
        compiler_params=pltpu.CompilerParams(vmem_limit_bytes=VMEM_BYTES),
        cost_estimate=pl.CostEstimate(
            flops=24 * count * depth * width,
            bytes_accessed=24 * count * depth * 4,
            transcendentals=2 * count * width,
        ),
        name="hidden_layer",
    )(places, rows, *first, *second)


def total_kernel(terms_ref, out_ref):
    out_ref[...] = jnp.sum(terms_ref[...].astype(jnp.float32), axis=0).astype(jnp.bfloat16)


def total_rows(terms):
    parts, count, block = terms.shape
    tile = count // 2
    return pl.pallas_call(
        total_kernel,
        grid=(count // tile,),
        in_specs=[pl.BlockSpec((parts, tile, block), lambda j: (0, j, 0))],
        out_specs=pl.BlockSpec((tile, block), lambda j: (j, 0)),
        out_shape=jax.ShapeDtypeStruct((count, block), jnp.bfloat16),
        name="total_rows",
    )(terms)


def join_kernel(pieces_ref, out_ref):
    parts, _, block = pieces_ref.shape
    for t in range(parts):
        out_ref[:, pl.ds(t * block, block)] = pieces_ref[t]


def join_columns(pieces):
    parts, group, block = pieces.shape
    return pl.pallas_call(
        join_kernel,
        out_shape=jax.ShapeDtypeStruct((group, parts * block), jnp.bfloat16),
        name="join_columns",
    )(pieces)


def weights_kernel(*refs):
    rows, acts = refs[0:4], refs[4:8]
    first_ref, second_ref = refs[8:10]
    first_ref[...] = sum(dot(rows[k][0], acts[k][1], 0, 0) for k in range(4)).astype(jnp.bfloat16)
    second_ref[...] = sum(dot(acts[k][0], rows[k][1], 0, 0) for k in range(4)).astype(jnp.bfloat16)


def weight_grads(rows, acts):
    _, _, count, depth = rows[0].shape
    width = acts[0].shape[2]
    return pl.pallas_call(
        weights_kernel,
        grid=(width // TILE,),
        in_specs=[pl.BlockSpec((None, 2, count, depth), lambda j: (0, 0, 0, 0))] * 4
        + [pl.BlockSpec((2, count, TILE), lambda j: (0, 0, j))] * 4,
        out_specs=[
            pl.BlockSpec((depth, TILE), lambda j: (0, j)),
            pl.BlockSpec((TILE, depth), lambda j: (j, 0)),
        ],
        out_shape=[
            jax.ShapeDtypeStruct((depth, width), jnp.bfloat16),
            jax.ShapeDtypeStruct((width, depth), jnp.bfloat16),
        ],
        compiler_params=pltpu.CompilerParams(vmem_limit_bytes=VMEM_BYTES),
        cost_estimate=pl.CostEstimate(
            flops=16 * count * depth * width,
            bytes_accessed=8 * 1024 * 1024,
            transcendentals=0,
        ),
        name="weight_grads",
    )(*rows, *acts)


def shards(tokens, routes, slots, gate, cotangent, w_in, w_out):
    experts = lax.axis_size("expert")
    parts = lax.axis_size("tensor")
    ring = lax.axis_size("dp")
    group, model_width = tokens.shape
    capacity = 2 * group // experts
    count = experts * capacity
    block = model_width // parts
    depth = model_width // ring
    halves = parts // ring
    replica = lax.axis_index("dp").astype(jnp.int32)
    y = lax.axis_index("tensor").astype(jnp.int32) % ring
    rings = [[i * ring + j for j in range(ring)] for i in range(halves)]

    start = (replica ^ y) * depth
    own_tokens = lax.dynamic_slice_in_dim(tokens, start, depth, 1)
    own_cotangent = lax.dynamic_slice_in_dim(cotangent, start, depth, 1)
    scaled = (own_cotangent.astype(jnp.float32) * gate[:, None]).astype(jnp.bfloat16)
    table = route_table(routes, slots, experts, capacity)
    sent_tokens = dot(table, own_tokens, 1, 0).astype(jnp.bfloat16)
    sent_grads = dot(table, scaled, 1, 0).astype(jnp.bfloat16)
    sent = jnp.concatenate(
        [
            sent_tokens.reshape(experts, capacity, depth),
            sent_grads.reshape(experts, capacity, depth),
        ],
        axis=1,
    )
    came = lax.all_to_all(sent, "expert", 0, 0, tiled=True)
    came = came.reshape(experts, 2, capacity, depth).transpose(1, 0, 2, 3)
    copies = jnp.broadcast_to(came.reshape(1, 2, count, depth), (ring, 2, count, depth))
    rows = lax.all_to_all(copies, "tensor", 0, 0, axis_index_groups=rings, tiled=True)

    first0, second0 = w_in[0], w_out[0]
    first2, second2 = lax.ppermute(first0, "dp", ACROSS), lax.ppermute(second0, "dp", ACROSS)
    first1, second1 = lax.ppermute(first0, "dp", BESIDE), lax.ppermute(second0, "dp", BESIDE)
    first3, second3 = lax.ppermute(first2, "dp", BESIDE), lax.ppermute(second2, "dp", BESIDE)

    order = jnp.arange(parts, dtype=jnp.int32)
    places = ((order // halves) ^ replica) * halves + order % halves
    acts0, partial_rows = hidden_layer(
        places, rows, (first0, first1, first2, first3), (second0, second1, second2, second3)
    )

    rows1 = lax.ppermute(rows[1:2], "dp", BESIDE)
    rows2 = lax.ppermute(rows[2:3], "dp", ACROSS)
    rows3 = lax.ppermute(lax.ppermute(rows[3:4], "dp", ACROSS), "dp", BESIDE)
    acts1 = lax.ppermute(acts0, "dp", BESIDE)
    acts2 = lax.ppermute(acts0, "dp", ACROSS)
    partial_rows, rows2 = lax.optimization_barrier((partial_rows, rows2))
    terms = lax.all_to_all(partial_rows, "tensor", 0, 0, tiled=True)
    row_grads = total_rows(terms)
    returned = lax.all_to_all(
        row_grads.reshape(experts, capacity, block), "expert", 0, 0, tiled=True
    ).reshape(count, block)
    own_grads = dot(table, returned, 0, 0).astype(jnp.bfloat16)
    own_grads, acts1, acts2, rows1, rows3 = lax.optimization_barrier(
        (own_grads, acts1, acts2, rows1, rows3)
    )
    acts3 = lax.ppermute(acts2, "dp", BESIDE)
    pieces = lax.all_to_all(
        jnp.broadcast_to(own_grads[None], (parts, group, block)), "tensor", 0, 0, tiled=True
    )
    grad_first, grad_second = weight_grads((rows, rows1, rows2, rows3), (acts0, acts1, acts2, acts3))
    pieces, grad_first, grad_second = lax.optimization_barrier((pieces, grad_first, grad_second))
    grad_tokens = join_columns(pieces)
    return grad_tokens, grad_first[None], grad_second[None]


def solution(mesh):
    return jax.shard_map(
        shards,
        mesh=mesh,
        in_specs=(
            P(("dp", "expert"), None),
            P(("dp", "expert")),
            P(("dp", "expert")),
            P(("dp", "expert")),
            P(("dp", "expert"), None),
            P("expert", "dp", "tensor"),
            P("expert", "tensor", "dp"),
        ),
        out_specs=(
            P(("dp", "expert"), None),
            P("expert", "dp", "tensor"),
            P("expert", "tensor", "dp"),
        ),
        check_vma=False,
    )
```

```python
import jax
import jax.numpy as jnp
from jax import lax
from jax.experimental import pallas as pl
from jax.experimental.pallas import tpu as pltpu
from jax.sharding import PartitionSpec as P

ACROSS = [(0, 2), (2, 0), (1, 3), (3, 1)]
BESIDE = [(0, 1), (1, 0), (2, 3), (3, 2)]
TILE = 1024
VMEM_BYTES = 24 * 1024 * 1024


def gelu_parts(preact):
    normal_cdf = 0.5 * (1.0 + lax.erf(preact * 0.7071067811865476))
    density = jnp.exp(-0.5 * preact * preact) * 0.3989422804014327
    return (preact * normal_cdf, normal_cdf + preact * density)


def route_table(routes, slots, rows, capacity):
    position = jnp.where(slots < capacity, routes * capacity + slots, -1)
    targets = lax.broadcasted_iota(jnp.int32, (rows, routes.shape[1]), 0)
    return jnp.where(targets == position, 1.0, 0.0).astype(jnp.bfloat16)


def dot(left, right, left_dim, right_dim):
    return lax.dot_general(
        left,
        right,
        (((left_dim,), (right_dim,)), ((), ())),
        preferred_element_type=jnp.float32,
    )


def dispatch_kernel(column_ref, routes_ref, slots_ref, gate_ref, tokens_ref, grads_ref, out_ref):
    experts, both, depth = out_ref.shape
    capacity = both // 2
    group = tokens_ref.shape[0]
    table = route_table(routes_ref[...], slots_ref[...], experts * capacity, capacity)
    across = lax.broadcasted_iota(jnp.int32, (group, group), 1)
    down = lax.broadcasted_iota(jnp.int32, (group, group), 0)
    gate = jnp.sum(jnp.where(across == down, gate_ref[...], 0.0), axis=1, keepdims=True)
    scaled = (grads_ref[...].astype(jnp.float32) * gate).astype(jnp.bfloat16)
    for place, values in ((0, tokens_ref[...]), (capacity, scaled)):
        sent = dot(table, values, 1, 0).astype(jnp.bfloat16)
        out_ref[:, pl.ds(place, capacity), :] = sent.reshape(experts, capacity, depth)


def dispatch(column, routes, slots, gate, tokens, cotangent, experts, capacity, depth):
    group = tokens.shape[0]
    row = pl.BlockSpec((1, group), lambda j, _: (0, 0))
    block = pl.BlockSpec((group, depth), lambda j, column: (0, column[0]))
    spec = pltpu.PrefetchScalarGridSpec(
        num_scalar_prefetch=1,
        grid=(1,),
        in_specs=[row] * 3 + [block] * 2,
        out_specs=pl.BlockSpec((experts, 2 * capacity, depth), lambda j, _: (0, 0, 0)),
    )
    return pl.pallas_call(
        dispatch_kernel,
        grid_spec=spec,
        out_shape=jax.ShapeDtypeStruct((experts, 2 * capacity, depth), jnp.bfloat16),
        name="dispatch",
    )(column, routes, slots, gate, tokens, cotangent)


def hidden_kernel(place_ref, rows_ref, *refs):
    first, second = refs[0:4], refs[4:8]
    acts_ref, sent_ref, total = refs[8:11]
    step, steps = pl.program_id(0), pl.num_programs(0)
    block = sent_ref.shape[2]
    halves = first[0].shape[0] // block

    preact = sum(dot(rows_ref[k, 0], first[k][...], 1, 0) for k in range(4))
    grad_hidden = sum(dot(rows_ref[k, 1], second[k][...], 1, 1) for k in range(4))
    value, slope = gelu_parts(preact)
    grad_pre = (grad_hidden * slope).astype(jnp.bfloat16)
    acts_ref[0] = value.astype(jnp.bfloat16)
    acts_ref[1] = grad_pre

    @pl.when(step == 0)
    def _():
        total[...] = jnp.zeros_like(total)

    for t in range(4 * halves):
        weight = first[t // halves][pl.ds((t % halves) * block, block), :]
        total[t] += dot(grad_pre, weight, 1, 1)

    @pl.when(step == steps - 1)
    def _():
        for t in range(4 * halves):
            sent_ref[place_ref[t]] = total[t].astype(jnp.bfloat16)


def hidden_layer(places, rows, first, second):
    _, _, count, depth = rows.shape
    width = first[0].shape[1]
    parts = places.shape[0]
    block = 4 * depth // parts
    spec = pltpu.PrefetchScalarGridSpec(
        num_scalar_prefetch=1,
        grid=(width // TILE,),
        in_specs=[pl.BlockSpec(rows.shape, lambda j, _: (0, 0, 0, 0))]
        + [pl.BlockSpec((depth, TILE), lambda j, _: (0, j))] * 4
        + [pl.BlockSpec((TILE, depth), lambda j, _: (j, 0))] * 4,
        out_specs=[
            pl.BlockSpec((2, count, TILE), lambda j, _: (0, 0, j)),
            pl.BlockSpec((parts, count, block), lambda j, _: (0, 0, 0)),
        ],
        scratch_shapes=[pltpu.VMEM((parts, count, block), jnp.float32)],
    )
    return pl.pallas_call(
        hidden_kernel,
        grid_spec=spec,
        out_shape=[
            jax.ShapeDtypeStruct((2, count, width), jnp.bfloat16),
            jax.ShapeDtypeStruct((parts, count, block), jnp.bfloat16),
        ],
        compiler_params=pltpu.CompilerParams(vmem_limit_bytes=VMEM_BYTES),
        cost_estimate=pl.CostEstimate(
            flops=24 * count * depth * width,
            bytes_accessed=24 * count * depth * 4,
            transcendentals=2 * count * width,
        ),
        name="hidden_layer",
    )(places, rows, *first, *second)


def total_kernel(terms_ref, out_ref):
    out_ref[...] = jnp.sum(terms_ref[...].astype(jnp.float32), axis=0).astype(jnp.bfloat16)


def total_rows(terms):
    parts, count, block = terms.shape
    tile = count // 2
    return pl.pallas_call(
        total_kernel,
        grid=(count // tile,),
        in_specs=[pl.BlockSpec((parts, tile, block), lambda j: (0, j, 0))],
        out_specs=pl.BlockSpec((tile, block), lambda j: (j, 0)),
        out_shape=jax.ShapeDtypeStruct((count, block), jnp.bfloat16),
        name="total_rows",
    )(terms)


def join_kernel(pieces_ref, out_ref):
    parts, _, block = pieces_ref.shape
    for t in range(parts):
        out_ref[:, pl.ds(t * block, block)] = pieces_ref[t]


def join_columns(pieces):
    parts, group, block = pieces.shape
    return pl.pallas_call(
        join_kernel,
        out_shape=jax.ShapeDtypeStruct((group, parts * block), jnp.bfloat16),
        name="join_columns",
    )(pieces)


def weights_kernel(*refs):
    rows, acts = refs[0:4], refs[4:8]
    first_ref, second_ref = refs[8:10]
    first_ref[...] = sum(dot(rows[k][0], acts[k][1], 0, 0) for k in range(4)).astype(jnp.bfloat16)
    second_ref[...] = sum(dot(acts[k][0], rows[k][1], 0, 0) for k in range(4)).astype(jnp.bfloat16)


def weight_grads(rows, acts):
    _, _, count, depth = rows[0].shape
    width = acts[0].shape[2]
    return pl.pallas_call(
        weights_kernel,
        grid=(width // TILE,),
        in_specs=[pl.BlockSpec((None, 2, count, depth), lambda j: (0, 0, 0, 0))] * 4
        + [pl.BlockSpec((2, count, TILE), lambda j: (0, 0, j))] * 4,
        out_specs=[
            pl.BlockSpec((depth, TILE), lambda j: (0, j)),
            pl.BlockSpec((TILE, depth), lambda j: (j, 0)),
        ],
        out_shape=[
            jax.ShapeDtypeStruct((depth, width), jnp.bfloat16),
            jax.ShapeDtypeStruct((width, depth), jnp.bfloat16),
        ],
        compiler_params=pltpu.CompilerParams(vmem_limit_bytes=VMEM_BYTES),
        cost_estimate=pl.CostEstimate(
            flops=16 * count * depth * width,
            bytes_accessed=8 * 1024 * 1024,
            transcendentals=0,
        ),
        name="weight_grads",
    )(*rows, *acts)


def shards(tokens, routes, slots, gate, cotangent, w_in, w_out):
    experts = lax.axis_size("expert")
    parts = lax.axis_size("tensor")
    ring = lax.axis_size("dp")
    group, model_width = tokens.shape
    capacity = 2 * group // experts
    count = experts * capacity
    block = model_width // parts
    depth = model_width // ring
    halves = parts // ring
    replica = lax.axis_index("dp").astype(jnp.int32)
    y = lax.axis_index("tensor").astype(jnp.int32) % ring
    rings = [[i * ring + j for j in range(ring)] for i in range(halves)]

    routes, slots, gate = (value.reshape(1, group) for value in (routes, slots, gate))
    column = (replica ^ y).reshape(1)
    sent = dispatch(column, routes, slots, gate, tokens, cotangent, experts, capacity, depth)
    came = lax.all_to_all(sent, "expert", 0, 0, tiled=True)
    came = came.reshape(experts, 2, capacity, depth).transpose(1, 0, 2, 3)
    copies = jnp.broadcast_to(came.reshape(1, 2, count, depth), (ring, 2, count, depth))
    rows = lax.all_to_all(copies, "tensor", 0, 0, axis_index_groups=rings, tiled=True)

    first0, second0 = w_in[0], w_out[0]
    first2, second2 = lax.ppermute(first0, "dp", ACROSS), lax.ppermute(second0, "dp", ACROSS)
    first1, second1 = lax.ppermute(first0, "dp", BESIDE), lax.ppermute(second0, "dp", BESIDE)
    first3, second3 = lax.ppermute(first2, "dp", BESIDE), lax.ppermute(second2, "dp", BESIDE)

    order = jnp.arange(parts, dtype=jnp.int32)
    places = ((order // halves) ^ replica) * halves + order % halves
    acts0, partial_rows = hidden_layer(
        places, rows, (first0, first1, first2, first3), (second0, second1, second2, second3)
    )

    rows1 = lax.ppermute(rows[1:2], "dp", BESIDE)
    rows2 = lax.ppermute(rows[2:3], "dp", ACROSS)
    rows3 = lax.ppermute(lax.ppermute(rows[3:4], "dp", ACROSS), "dp", BESIDE)
    acts1 = lax.ppermute(acts0, "dp", BESIDE)
    acts2 = lax.ppermute(acts0, "dp", ACROSS)
    partial_rows, rows2 = lax.optimization_barrier((partial_rows, rows2))
    terms = lax.all_to_all(partial_rows, "tensor", 0, 0, tiled=True)
    row_grads = total_rows(terms)
    returned = lax.all_to_all(
        row_grads.reshape(experts, capacity, block), "expert", 0, 0, tiled=True
    ).reshape(count, block)
    table = route_table(routes, slots, count, capacity)
    own_grads = dot(table, returned, 0, 0).astype(jnp.bfloat16)
    own_grads, acts1, acts2, rows1, rows3 = lax.optimization_barrier(
        (own_grads, acts1, acts2, rows1, rows3)
    )
    acts3 = lax.ppermute(acts2, "dp", BESIDE)
    pieces = lax.all_to_all(
        jnp.broadcast_to(own_grads[None], (parts, group, block)), "tensor", 0, 0, tiled=True
    )
    grad_first, grad_second = weight_grads((rows, rows1, rows2, rows3), (acts0, acts1, acts2, acts3))
    pieces, grad_first, grad_second = lax.optimization_barrier((pieces, grad_first, grad_second))
    grad_tokens = join_columns(pieces)
    return grad_tokens, grad_first[None], grad_second[None]


def solution(mesh):
    return jax.shard_map(
        shards,
        mesh=mesh,
        in_specs=(
            P(("dp", "expert"), None),
            P(("dp", "expert")),
            P(("dp", "expert")),
            P(("dp", "expert")),
            P(("dp", "expert"), None),
            P("expert", "dp", "tensor"),
            P("expert", "tensor", "dp"),
        ),
        out_specs=(
            P(("dp", "expert"), None),
            P("expert", "dp", "tensor"),
            P("expert", "tensor", "dp"),
        ),
        check_vma=False,
    )
```
